128 devices in a mesh: pipe: 4 (over z_hi, core), expert: 32 (over x, y, z_lo).
Axes of the slice: x: 4, y: 4, z: 4 (z_hi: 2, z_lo: 2; z = z_hi * 2 + z_lo), core: 2. Of those that a mesh axis runs over, the one named last changes fastest.
Arguments:
- layer_input: bfloat16 [4, 4096, 7168], P('pipe', 'expert'), may hold values from -6 to 6
- out_grad: bfloat16 [4, 4096, 7168], P('pipe', 'expert'), may hold values from -6 to 6
- route_ids: int32 [4, 4096, 8], P('pipe', 'expert'), may hold values from 0 to 255, as said below
- route_gates: float32 [4, 4096, 8], P('pipe', 'expert'), may hold values from 0.2 to 1.2
- gate_weight: bfloat16 [4, 32, 7168, 256], P('pipe', 'expert'), may hold values from -0.0625 to 0.0625
- up_weight: bfloat16 [4, 32, 7168, 256], P('pipe', 'expert'), may hold values from -0.0625 to 0.0625
- down_weight: bfloat16 [4, 32, 256, 7168], P('pipe', 'expert'), may hold values from -0.125 to 0.125
- head_grad: bfloat16 [4096, 7168], P('expert'), may hold values from -6 to 6
Outputs:
- next_grad: bfloat16 [4, 4096, 7168], P('pipe', 'expert')
- gate_grad: float32 [4, 4096, 8], P('pipe', 'expert')
The draws below stay inside these ranges and needn't reach their ends.
Inputs may be any that keep to these rules, and one draw needn't show every extreme that they name: `route_ids`: ids of one token are distinct. In each section and in the rows of one device, at most 16 tokens name any one expert below 4; in each section some such expert is named by exactly 16 tokens in the rows of every device.
All inputs are finite; a program needn't handle non-finite values.
Results may differ from the reference program's by a relative error of at most 0.0059.
Values may be sent and summed in bfloat16 or wider, within the bound.
No kernel may reach another device: no remote copies, remote signals or barrier semaphores. Data moves between devices by JAX's collectives and lax.ppermute only.
A program may use at most 128 MiB of HBM per device.

```python
import jax
import jax.numpy as jnp
from jax import lax

D = 7168
FF = 2048
ROUTED = 256
TOP = 8
SLICES = 8
TOK_DEV = 128
SECTIONS = 4
EXPERTS = 4
FH = 256
HOLDERS = 32
CAP = 16
TOKENS = 4096


def draw_route_ids(key, part):
    key = jax.random.fold_in(key, 7)
    keys = jax.random.split(key, 5)
    blocks = TOKENS // TOK_DEV
    counts = jax.random.randint(keys[0], (SECTIONS, blocks, EXPERTS), CAP // 3, CAP + 1)
    hottest = jax.random.randint(keys[1], (SECTIONS, 1, 1), 0, EXPERTS)
    counts = jnp.where(jnp.arange(EXPERTS)[None, None, :] == hottest, CAP, counts)
    scores = jax.random.randint(keys[2], (SECTIONS, blocks, EXPERTS, TOK_DEV), 0, 2 ** 16) * TOK_DEV + jnp.arange(TOK_DEV)
    ranks = jnp.argsort(jnp.argsort(scores, axis=-1), axis=-1)
    chosen = (ranks < counts[..., None]).astype(jnp.int32)
    chosen = jnp.transpose(chosen, (0, 1, 3, 2))
    order = jnp.cumsum(chosen, axis=-1) - 1
    total = jnp.sum(chosen, axis=-1, keepdims=True)
    places = jnp.arange(TOP)
    matches = (chosen[..., None, :] == 1) & (order[..., None, :] == places[:, None])
    inside = jnp.sum(jnp.where(matches, jnp.arange(EXPERTS), 0), axis=-1)
    spare = ROUTED - EXPERTS
    other_scores = jax.random.randint(keys[3], (SECTIONS, blocks, TOK_DEV, spare), 0, 2 ** 16) * spare + jnp.arange(spare)
    outside = lax.top_k(other_scores, TOP)[1] + EXPERTS
    merged = jnp.where(places < total, inside, outside)
    shuffle = jax.random.randint(keys[4], (SECTIONS, blocks, TOK_DEV, TOP), 0, 2 ** 16) * TOP + places
    merged = jnp.take_along_axis(merged, jnp.argsort(shuffle, axis=-1), axis=-1)
    return merged.reshape(SECTIONS, TOKENS, TOP).astype(jnp.int32)


def block_scale(stream_key, shape, cuts, least, largest):
    loudness, own = 1.0, jax.random.fold_in(stream_key, 6)
    for position, shards_of in cuts:
        draws = jnp.exp(jax.random.uniform(jax.random.fold_in(own, position), (shards_of,), jnp.float32, least / len(cuts), largest / len(cuts)))
        loudness = loudness * jnp.repeat(draws, shape[position] // shards_of).reshape([-1 if axis == position else 1 for axis in range(len(shape))])
    return loudness


def scatter_about(stream_key, dims, width, limit, shards=(), kind=jnp.bfloat16):
    entries = width * jax.random.normal(stream_key, dims, jnp.float32)
    if shards:
        entries = entries * block_scale(stream_key, dims, shards, -0.22, 0.18)
    return jnp.clip(entries, -limit, limit).astype(kind)


def setup_inputs(seed: int = 0) -> dict:
    streams_of = jax.random.split(jax.random.key(seed), 9)
    layer_input = scatter_about(streams_of[0], (SECTIONS, TOKENS, D), 1.0, 6.0, ((0, 4), (1, 32)))
    out_grad = scatter_about(streams_of[1], (SECTIONS, TOKENS, D), 1.0, 6.0, ((0, 4), (1, 32)))
    route_ids = draw_route_ids(jax.random.fold_in(streams_of[8], 71), 0)
    route_gates = jnp.clip(0.2 + 1 * jax.random.uniform(streams_of[3], (SECTIONS, TOKENS, TOP), jnp.float32) ** block_scale(streams_of[3], (SECTIONS, TOKENS, TOP), ((0, 4), (1, 32)), -0.2, 0.2), 0.2, 1.2)
    gate_weight = scatter_about(streams_of[4], (SECTIONS, HOLDERS, D, FH), D ** -0.5, 0.0625, ((0, 4), (1, 32)))
    up_weight = scatter_about(streams_of[5], (SECTIONS, HOLDERS, D, FH), D ** -0.5, 0.0625, ((0, 4), (1, 32)))
    down_weight = scatter_about(streams_of[6], (SECTIONS, HOLDERS, FH, D), FF ** -0.5, 0.125, ((0, 4), (1, 32)))
    head_grad = scatter_about(streams_of[7], (TOKENS, D), 1.0, 6.0, ((0, 32),))
    return dict(layer_input=layer_input, out_grad=out_grad, route_ids=route_ids, route_gates=route_gates, gate_weight=gate_weight, up_weight=up_weight, down_weight=down_weight, head_grad=head_grad)


def slice_backward(rows_in, rows_grad, gate_mat, up_mat, down_mat):
    gate_pre = jnp.dot(rows_in, gate_mat, preferred_element_type=jnp.float32)
    up_pre = jnp.dot(rows_in, up_mat, preferred_element_type=jnp.float32)
    sigma = jax.nn.sigmoid(gate_pre)
    swish = gate_pre * sigma
    hidden = swish * up_pre
    hidden_grad = lax.dot_general(rows_grad, down_mat, (((1,), (1,)), ((), ())), preferred_element_type=jnp.float32)
    score = jnp.sum(hidden * hidden_grad, axis=1)
    gate_back = (hidden_grad * up_pre * sigma * (1.0 + gate_pre * (1.0 - sigma))).astype(jnp.bfloat16)
    up_back = (hidden_grad * swish).astype(jnp.bfloat16)
    term = lax.dot_general(gate_back, gate_mat, (((1,), (1,)), ((), ())), preferred_element_type=jnp.float32)
    term = term + lax.dot_general(up_back, up_mat, (((1,), (1,)), ((), ())), preferred_element_type=jnp.float32)
    return term.astype(jnp.bfloat16), score.astype(jnp.bfloat16)


def section_backward(tokens, grads, routes, gates, gate_all, up_all, down_all):
    blocks = TOKENS // TOK_DEV
    named = routes[:, :, None] == jnp.arange(EXPERTS, dtype=jnp.int32)[None, None, :]
    hits = jnp.any(named, axis=1).astype(jnp.int32).reshape(blocks, TOK_DEV, EXPERTS)
    places = jnp.cumsum(hits, axis=1) - hits
    chosen = (places[:, :, :, None] == jnp.arange(CAP, dtype=jnp.int32)) & (hits[:, :, :, None] == 1)
    chosen = chosen.astype(jnp.float32)
    token_blocks = tokens.astype(jnp.float32).reshape(blocks, TOK_DEV, D)
    grad_blocks = grads.astype(jnp.float32).reshape(blocks, TOK_DEV, D)
    token_rows = jnp.einsum('ntec,ntd->necd', chosen, token_blocks, precision=lax.Precision.HIGHEST).astype(jnp.bfloat16)
    grad_rows = jnp.einsum('ntec,ntd->necd', chosen, grad_blocks, precision=lax.Precision.HIGHEST).astype(jnp.bfloat16)
    summed = []
    scored = []
    for expert in range(EXPERTS):
        rows_in = token_rows[:, expert].reshape(blocks * CAP, D)
        rows_grad = grad_rows[:, expert].reshape(blocks * CAP, D)
        total = jnp.zeros((blocks * CAP, D), jnp.float32)
        total_score = jnp.zeros((blocks * CAP,), jnp.float32)
        for piece in range(SLICES):
            holder = expert * SLICES + piece
            term, score = slice_backward(rows_in, rows_grad, gate_all[holder], up_all[holder], down_all[holder])
            total = total + term.astype(jnp.float32)
            total_score = total_score + score.astype(jnp.float32)
        summed.append(total.reshape(blocks, CAP, D))
        scored.append(total_score.reshape(blocks, CAP))
    sums = jnp.stack(summed, axis=1)
    totals = jnp.stack(scored, axis=1)
    weighted_gate = jnp.sum(gates[:, :, None] * named.astype(jnp.float32), axis=1).reshape(blocks, TOK_DEV, EXPERTS)
    mixing = chosen * weighted_gate[:, :, :, None]
    moe_grad = jnp.einsum('ntec,necd->ntd', mixing, sums, precision=lax.Precision.HIGHEST).reshape(TOKENS, D)
    passed = (grads.astype(jnp.float32) + moe_grad).astype(jnp.bfloat16)
    token_scores = jnp.einsum('ntec,nec->nte', chosen, totals, precision=lax.Precision.HIGHEST).reshape(TOKENS, EXPERTS)
    gate_grad = jnp.sum(named.astype(jnp.float32) * token_scores[:, None, :], axis=2)
    return passed, gate_grad


def reference(layer_input, out_grad, route_ids, route_gates, gate_weight, up_weight, down_weight, head_grad):
    passed_all = []
    gate_all = []
    for section in range(SECTIONS):
        passed, gate_grad = section_backward(layer_input[section], out_grad[section], route_ids[section], route_gates[section], gate_weight[section], up_weight[section], down_weight[section])
        passed_all.append(passed)
        gate_all.append(gate_grad)
    next_grad = jnp.stack(passed_all[1:] + [head_grad], axis=0)
    return next_grad, jnp.stack(gate_all, axis=0)
```

```python
import jax
import jax.numpy as jnp
from jax import lax
from jax.sharding import PartitionSpec as P

SLICES = 8
CAP = 16
NX, NY, NZ = 4, 4, 2
BLOCKS = [(dy, dz) for dz in range(NZ) for dy in range(NY)]


def place(x, y, z):
    return ((x % NX) * NY + y % NY) * NZ + z % NZ


def send(block, dx=0, dy=0, dz=0, back=0):
    route = []
    for x in range(NX):
        for y in range(NY):
            for z in range(NZ):
                route.append((place(x, y, z), place(x + dx, y + dy, z + dz)))
    if not back:
        return lax.ppermute(block, "expert", route)
    size = NX * NY * NZ
    route = [
        (p * size + i, (p - back) * size + j)
        for p in range(back, lax.axis_size("pipe"))
        for i, j in route
    ]
    return lax.ppermute(block, ("pipe", "expert"), route)


def plane_gather(first, flip):
    width = first[0].shape[-1]

    def joined(parts, s):
        return jnp.stack([part[s] for part in parts])

    rows_z = [send(part, dz=1) for part in first]
    rows_p = [send(part, dy=1) for part in first]
    rows_m = [send(part, dy=-1) for part in first]
    ins, grads = {}, {}
    for key, parts in (((0, 0), first), ((0, 1), rows_z), ((3, 0), rows_p), ((1, 0), rows_m)):
        ins[key] = joined(parts, 0)
        grads[key] = joined(parts, 1)
    ins[2, 0] = send(ins[3, 0], dy=1)
    grads[2, 0] = send(grads[1, 0], dy=-1)
    ins[3, 1] = send(ins[0, 1], dy=1)
    ins[1, 1] = send(ins[0, 1], dy=-1)
    grads[3, 1] = send(grads[3, 0], dz=1)
    grads[1, 1] = send(grads[1, 0], dz=1)
    grads[2, 1] = send(grads[2, 0], dz=1)
    ins[2, 1] = send(ins[1, 1], dy=-1) if flip else send(ins[3, 1], dy=1)
    return (
        jnp.concatenate([ins[k] for k in BLOCKS]).reshape(-1, width),
        jnp.concatenate([grads[k] for k in BLOCKS]).reshape(-1, width),
    )


def slice_backward(rows_in, rows_grad, gate_mat, up_mat, down_mat, piece):
    gate_pre = jnp.dot(rows_in, gate_mat, preferred_element_type=jnp.float32)
    up_pre = jnp.dot(rows_in, up_mat, preferred_element_type=jnp.float32)
    sigma = jax.nn.sigmoid(gate_pre)
    swish = gate_pre * sigma
    hidden = swish * up_pre
    hidden_grad = lax.dot_general(
        rows_grad, down_mat, (((1,), (1,)), ((), ())), preferred_element_type=jnp.float32
    )
    score = jnp.sum(hidden * hidden_grad, axis=1)
    gate_back = (hidden_grad * up_pre * sigma * (1.0 + gate_pre * (1.0 - sigma))).astype(
        jnp.bfloat16
    )
    up_back = (hidden_grad * swish).astype(jnp.bfloat16)
    term = lax.dot_general(
        gate_back, gate_mat, (((1,), (1,)), ((), ())), preferred_element_type=jnp.float32
    )
    term = term + lax.dot_general(
        up_back, up_mat, (((1,), (1,)), ((), ())), preferred_element_type=jnp.float32
    )
    own = jnp.arange(128, dtype=jnp.int32)[None, :] == piece
    marked = jnp.where(own, score[:, None], 0.0)
    return jnp.concatenate([term.astype(jnp.bfloat16), marked.astype(jnp.bfloat16)], axis=1)


def added(*parts):
    total = parts[0].astype(jnp.float32)
    for part in parts[1:]:
        total = total + part.astype(jnp.float32)
    return total.astype(jnp.bfloat16)


def plane_reduce(terms):
    width = terms.shape[-1]
    terms = terms.reshape(len(BLOCKS), 2, CAP, width)
    late = {k: terms[i, 0] for i, k in enumerate(BLOCKS)}
    soon = {k: terms[i, 1] for i, k in enumerate(BLOCKS)}
    cross = send(terms[NY:, 1], dz=1)
    far_p = send(late[2, 0], dy=1)
    far_m = send(late[2, 1], dy=-1)
    sums = {dy: added(soon[dy, 0], cross[dy]) for dy in range(NY)}
    near_p = send(jnp.stack([added(late[1, 0], far_p), late[1, 1]]), dy=1)
    near_m = send(jnp.stack([late[3, 0], added(late[3, 1], far_m)]), dy=-1)
    half = CAP // 2
    away_p = send(sums[2][:half], dy=1)
    away_m = send(sums[2][half:], dy=-1)
    other = added(late[0, 1], near_p[1], near_m[1])
    last = send(other, dz=1)
    next_p = send(
        jnp.concatenate([added(sums[1][:half], away_p), sums[1][half:]]), dy=1
    )
    next_m = send(
        jnp.concatenate([sums[3][:half], added(sums[3][half:], away_m)]), dy=-1
    )
    return (
        added(late[0, 0], near_p[0], near_m[0], last),
        added(sums[0], next_p, next_m),
    )


def body(
    layer_input, out_grad, route_ids, route_gates, gate_weight, up_weight, down_weight, head_grad
):
    holder = lax.axis_index("expert")
    piece = holder % SLICES
    group = holder // SLICES
    tokens = layer_input[0]
    grads = out_grad[0]
    routes = route_ids[0]
    gates = route_gates[0]
    gate_mat = gate_weight[0, 0]
    up_mat = up_weight[0, 0]
    down_mat = down_weight[0, 0]
    width = tokens.shape[1]
    order = (jnp.arange(NX, dtype=jnp.int32) + group) % NX
    named = routes[:, :, None] == order[None, None, :]
    hits = jnp.any(named, axis=1).astype(jnp.int32)
    places = jnp.cumsum(hits, axis=0) - hits
    chosen = (places[:, :, None] == jnp.arange(CAP, dtype=jnp.int32)) & (hits[:, :, None] == 1)
    picker = chosen.astype(jnp.bfloat16)
    token_rows = jnp.einsum(
        "tec,td->ecd", picker, tokens, preferred_element_type=jnp.float32
    ).astype(jnp.bfloat16)
    grad_rows = jnp.einsum("tec,td->ecd", picker, grads, preferred_element_type=jnp.float32).astype(
        jnp.bfloat16
    )
    rows = [jnp.stack([token_rows[dx], grad_rows[dx]]) for dx in range(NX)]
    arrived = [rows[0]] + [send(rows[dx], dx=dx) for dx in range(1, NX)]

    weighted_gate = jnp.sum(gates[:, :, None] * named.astype(jnp.float32), axis=1)
    chosen_float = chosen.astype(jnp.float32)
    mixing = (chosen_float * weighted_gate[:, :, None]).reshape(-1, NX * CAP)
    mixing_back = send(mixing, back=1)
    grads_back = send(grads, back=1)

    chunks = [arrived[:2], [jnp.stack([arrived[2][s], arrived[3][s]]) for s in range(2)]]
    results = []
    for c in range(2):
        if c == 0:
            ins, gs = plane_gather(arrived[:2], False)
        else:
            ins, gs = plane_gather(arrived[2:], True)
        terms = slice_backward(ins, gs, gate_mat, up_mat, down_mat, piece)
        results.extend(plane_reduce(terms))
    scores, moved = [], []
    for dx in range(NX):
        part = results[dx]
        marks = part[:, width:]
        scores.append(send(marks, dx=-dx) if dx else marks)
        moved.append(send(part[:, :width], dx=-dx, back=1))
    sums = jnp.concatenate(moved)
    high = lax.reduce_precision(mixing_back, 8, 7)
    low = mixing_back - high
    moe_grad = jnp.dot(
        high.astype(jnp.bfloat16), sums, preferred_element_type=jnp.float32
    ) + jnp.dot(low.astype(jnp.bfloat16), sums, preferred_element_type=jnp.float32)
    passed = (grads_back.astype(jnp.float32) + moe_grad).astype(jnp.bfloat16)
    last_section = lax.axis_index("pipe") == lax.axis_size("pipe") - 1
    next_grad = jnp.where(last_section, head_grad, passed)
    totals = jnp.sum(jnp.stack(scores).astype(jnp.float32), axis=2)
    token_scores = jnp.sum(chosen_float * totals[None], axis=2)
    gate_grad = jnp.sum(named.astype(jnp.float32) * token_scores[:, None, :], axis=2)
    return (next_grad[None], gate_grad[None])


def solution(mesh):
    in_specs = (
        P("pipe", "expert", None),
        P("pipe", "expert", None),
        P("pipe", "expert", None),
        P("pipe", "expert", None),
        P("pipe", "expert", None, None),
        P("pipe", "expert", None, None),
        P("pipe", "expert", None, None),
        P("expert", None),
    )
    out_specs = (P("pipe", "expert", None), P("pipe", "expert", None))
    return jax.shard_map(body, mesh=mesh, in_specs=in_specs, out_specs=out_specs, check_vma=False)
```

```python
import jax
import jax.numpy as jnp
from jax import lax
from jax.sharding import PartitionSpec as P

CAP = 16
MARKS = 128
NX, NY, NZ = 4, 4, 2
TIED = ()
BLOCKS = [(dy, dz) for dz in range(NZ) for dy in range(NY)]
PLUS, MINUS, CROSS = dict(dy=1), dict(dy=-1), dict(dz=1)


def place(x, y, z):
    return ((x % NX) * NY + y % NY) * NZ + z % NZ


def send(block, dx=0, dy=0, dz=0, back=0):
    route = []
    for x in range(NX):
        for y in range(NY):
            for z in range(NZ):
                route.append((place(x, y, z), place(x + dx, y + dy, z + dz)))
    if not back:
        return lax.ppermute(block, "expert", route)
    size = NX * NY * NZ
    route = [
        (p * size + i, (p - back) * size + j)
        for p in range(back, lax.axis_size("pipe"))
        for i, j in route
    ]
    return lax.ppermute(block, ("pipe", "expert"), route)


class Links:
    def __init__(self):
        self.phase = 0
        self.due = {}
        self.queue = {}

    def add(self, block, held, key, lag=1, **hop):
        kind = (tuple(sorted(hop.items())), lag, block.dtype, block.shape[-1])
        group = self.queue.setdefault(kind, [])
        group.append((block, held, key))

    def run(self, others=()):
        groups = list(self.queue.items())
        blocks = [
            jnp.concatenate([b for b, _, _ in moves]) if len(moves) > 1 else moves[0][0]
            for _, moves in groups
        ]
        self.last = []
        blocks, _ = lax.optimization_barrier(
            (blocks, self.due.pop(self.phase, []) + list(others))
        )
        for block, ((hop, lag, _, _), moves) in zip(blocks, groups):
            result = send(block, **dict(hop))
            self.due.setdefault(self.phase + lag, []).append(result)
            if lag == 1:
                self.last.append(result)
            start = 0
            for sent, held, key in moves:
                rows = sent.shape[0]
                held[key] = result[start : start + rows]
                start += rows
        self.phase += 1
        self.queue = {}


class Spread:
    def __init__(self):
        self.rows, self.ins, self.grads = {}, {}, {}

    def both(self, key):
        self.ins[key], self.grads[key] = self.rows[key][:CAP], self.rows[key][CAP:]

    def first(self, links):
        rows = self.rows
        self.both((0, 0))
        links.add(rows[0, 0], rows, (3, 0), **PLUS)
        links.add(rows[0, 0], rows, (1, 0), **MINUS)
        links.add(rows[0, 0], rows, (0, 1), **CROSS)

    def second(self, links):
        ins, grads = self.ins, self.grads
        for key in ((3, 0), (1, 0), (0, 1)):
            self.both(key)
        links.add(ins[3, 0], ins, (2, 0), **PLUS)
        links.add(ins[0, 1], ins, (3, 1), **PLUS)
        links.add(grads[1, 0], grads, (2, 0), **MINUS)
        links.add(ins[0, 1], ins, (1, 1), **MINUS)
        links.add(grads[1, 0], grads, (1, 1), **CROSS)
        links.add(grads[3, 0], grads, (3, 1), **CROSS)

    def third(self, links):
        links.add(self.ins[3, 1], self.ins, (2, 1), **PLUS)
        links.add(self.grads[1, 1], self.grads, (2, 1), **MINUS)


def added(*parts):
    total = parts[0].astype(jnp.float32)
    for part in parts[1:]:
        total = total + part.astype(jnp.float32)
    return total.astype(jnp.bfloat16)


class LateCross:
    def __init__(self, terms):
        self.terms, self.got = terms, {}

    def first(self, links):
        links.add(self.terms[2, 0], self.got, "far+", **PLUS)
        links.add(self.terms[2, 1], self.got, "far-", **MINUS)

    def second(self, links):
        terms, got = self.terms, self.got
        links.add(added(terms[1, 0], got["far+"]), got, "a+", **PLUS)
        links.add(terms[1, 1], got, "b+", **PLUS)
        links.add(terms[3, 0], got, "a-", **MINUS)
        links.add(added(terms[3, 1], got["far-"]), got, "b-", **MINUS)

    def third(self, links):
        got = self.got
        links.add(added(self.terms[0, 1], got["b+"], got["b-"]), got, "z", **CROSS)

    def total(self):
        got = self.got
        return added(self.terms[0, 0], got["a+"], got["a-"], got["z"])


class SoonCross:
    def __init__(self, terms):
        self.terms, self.got = terms, {}

    def first(self, links):
        for dy in range(NY):
            links.add(self.terms[dy, 1], self.got, dy, **CROSS)

    def second(self, links):
        got = self.got
        half = CAP // 2
        self.sums = [added(self.terms[dy, 0], got[dy]) for dy in range(NY)]
        links.add(self.sums[2][:half], got, "far+", **PLUS)
        links.add(self.sums[2][half:], got, "far-", **MINUS)

    def third(self, links):
        sums, got = self.sums, self.got
        half = CAP // 2
        links.add(
            jnp.concatenate([added(sums[1][:half], got["far+"]), sums[1][half:]]),
            got,
            "+",
            **PLUS,
        )
        links.add(
            jnp.concatenate([sums[3][:half], added(sums[3][half:], got["far-"])]),
            got,
            "-",
            **MINUS,
        )

    def total(self):
        return added(self.sums[0], self.got["+"], self.got["-"])


def slice_backward(rows_in, rows_grad, gate_mat, up_mat, down_mat, piece):
    gate_pre = jnp.dot(rows_in, gate_mat, preferred_element_type=jnp.float32)
    up_pre = jnp.dot(rows_in, up_mat, preferred_element_type=jnp.float32)
    sigma = jax.nn.sigmoid(gate_pre)
    swish = gate_pre * sigma
    hidden = swish * up_pre
    hidden_grad = lax.dot_general(
        rows_grad, down_mat, (((1,), (1,)), ((), ())), preferred_element_type=jnp.float32
    )
    score = jnp.sum(hidden * hidden_grad, axis=1)
    gate_back = (hidden_grad * up_pre * sigma * (1.0 + gate_pre * (1.0 - sigma))).astype(
        jnp.bfloat16
    )
    up_back = (hidden_grad * swish).astype(jnp.bfloat16)
    term = lax.dot_general(
        gate_back, gate_mat, (((1,), (1,)), ((), ())), preferred_element_type=jnp.float32
    )
    term = term + lax.dot_general(
        up_back, up_mat, (((1,), (1,)), ((), ())), preferred_element_type=jnp.float32
    )
    own = jnp.arange(MARKS, dtype=jnp.int32)[None, :] == piece
    marks = jnp.where(own, score[:, None], 0.0)
    return jnp.concatenate([term.astype(jnp.bfloat16), marks.astype(jnp.bfloat16)], axis=1)


def body(
    layer_input, out_grad, route_ids, route_gates, gate_weight, up_weight, down_weight, head_grad
):
    holder = lax.axis_index("expert")
    group = holder // (NY * NZ)
    tokens = layer_input[0]
    width = tokens.shape[1]
    grads = out_grad[0]
    routes = route_ids[0]
    gates = route_gates[0]
    weights = gate_weight[0, 0], up_weight[0, 0], down_weight[0, 0]
    order = (jnp.arange(NX, dtype=jnp.int32) + group) % NX
    named = routes[:, :, None] == order[None, None, :]
    hits = jnp.any(named, axis=1).astype(jnp.int32)
    places = jnp.cumsum(hits, axis=0) - hits
    chosen = (places[:, :, None] == jnp.arange(CAP, dtype=jnp.int32)) & (hits[:, :, None] == 1)
    picker = chosen.astype(jnp.bfloat16)
    token_rows = jnp.einsum(
        "tec,td->ecd", picker, tokens, preferred_element_type=jnp.float32
    ).astype(jnp.bfloat16)
    grad_rows = jnp.einsum("tec,td->ecd", picker, grads, preferred_element_type=jnp.float32).astype(
        jnp.bfloat16
    )
    weighted_gate = jnp.sum(gates[:, :, None] * named.astype(jnp.float32), axis=1)
    chosen_float = chosen.astype(jnp.float32)
    mixing = (chosen_float * weighted_gate[:, :, None]).reshape(-1, NX * CAP)

    units = [Spread() for _ in range(NX)]
    rows = [jnp.concatenate([token_rows[dx], grad_rows[dx]]) for dx in range(NX)]
    back, moved, scores = {}, {}, {}
    units[0].rows[0, 0] = rows[0]
    for dx in (1, 3):
        units[dx].rows[0, 0] = send(rows[dx], dx=dx)

    def compute(dxs, kinds):
        ins = jnp.concatenate([units[dx].ins[k] for dx in dxs for k in BLOCKS])
        gs = jnp.concatenate([units[dx].grads[k] for dx in dxs for k in BLOCKS])
        term = slice_backward(ins, gs, *weights, holder % (NY * NZ))
        term = term.reshape(len(dxs), len(BLOCKS), CAP, -1)
        return [
            kind({k: term[i, n] for n, k in enumerate(BLOCKS)}) for i, kind in enumerate(kinds)
        ]

    def home(links, dx, reduced):
        part = reduced.total()
        marks = part[:, width:]
        if dx:
            links.add(marks, scores, dx, dx=-dx)
        else:
            scores[dx] = marks
        links.add(part[:, :width], moved, dx, dx=-dx, back=1)

    def chain(dxs):
        links = Links()
        one, two = (units[dx] for dx in dxs)
        one.first(links)
        if 2 in dxs:
            links.add(rows[2], units[2].rows, (0, 0), dx=2)
        yield links
        two.first(links)
        one.second(links)
        if 0 in dxs:
            links.add(grads, back, "grads", lag=3, back=1)
            links.add(mixing, back, "mixing", lag=3, back=1)
        yield links
        two.second(links)
        one.third(links)
        yield links
        two.third(links)
        yield links
        sums = compute(dxs, [LateCross, SoonCross])
        for part in sums:
            part.first(links)
        yield links
        for part in sums:
            part.second(links)
        yield links
        for part in sums:
            part.third(links)
        yield links
        for dx, part in zip(dxs, sums):
            home(links, dx, part)
        yield links

    for phase, (early, late) in enumerate(zip(chain((0, 1)), chain((3, 2)))):
        early.run()
        late.run(early.last if phase in TIED else ())

    sums = jnp.concatenate([moved[dx] for dx in range(NX)])
    high = lax.reduce_precision(back["mixing"], 8, 7)
    low = back["mixing"] - high
    moe_grad = jnp.dot(
        high.astype(jnp.bfloat16), sums, preferred_element_type=jnp.float32
    ) + jnp.dot(low.astype(jnp.bfloat16), sums, preferred_element_type=jnp.float32)
    passed = (back["grads"].astype(jnp.float32) + moe_grad).astype(jnp.bfloat16)
    last_section = lax.axis_index("pipe") == lax.axis_size("pipe") - 1
    next_grad = jnp.where(last_section, head_grad, passed)

    totals = jnp.sum(jnp.stack([scores[dx] for dx in range(NX)]).astype(jnp.float32), axis=2)
    token_scores = jnp.sum(chosen_float * totals[None], axis=2)
    gate_grad = jnp.sum(named.astype(jnp.float32) * token_scores[:, None, :], axis=2)
    return (next_grad[None], gate_grad[None])


def solution(mesh):
    in_specs = (
        P("pipe", "expert", None),
        P("pipe", "expert", None),
        P("pipe", "expert", None),
        P("pipe", "expert", None),
        P("pipe", "expert", None, None),
        P("pipe", "expert", None, None),
        P("pipe", "expert", None, None),
        P("expert", None),
    )
    out_specs = (P("pipe", "expert", None), P("pipe", "expert", None))
    return jax.shard_map(body, mesh=mesh, in_specs=in_specs, out_specs=out_specs, check_vma=False)
```

```python
import jax
import jax.numpy as jnp
from jax import lax
from jax.experimental import pallas as pl
from jax.experimental.pallas import tpu as pltpu
from jax.sharding import PartitionSpec as P

CAP = 16
MARKS = 128
NX, NY, NZ = 4, 4, 2
TIED = ()
FLOPS = 40
BLEND = 25000000000
VMEM = pl.BlockSpec(memory_space=pltpu.VMEM)
SMEM = pl.BlockSpec(memory_space=pltpu.SMEM)
BLOCKS = [(dy, dz) for dz in range(NZ) for dy in range(NY)]
PLUS, MINUS, CROSS = dict(dy=1), dict(dy=-1), dict(dz=1)


def place(x, y, z):
    return ((x % NX) * NY + y % NY) * NZ + z % NZ


def send(block, dx=0, dy=0, dz=0, back=0):
    route = []
    for x in range(NX):
        for y in range(NY):
            for z in range(NZ):
                route.append((place(x, y, z), place(x + dx, y + dy, z + dz)))
    if not back:
        return lax.ppermute(block, "expert", route)
    size = NX * NY * NZ
    route = [
        (p * size + i, (p - back) * size + j)
        for p in range(back, lax.axis_size("pipe"))
        for i, j in route
    ]
    return lax.ppermute(block, ("pipe", "expert"), route)


class Rows:
    def __init__(self, array, start, rows):
        self.array, self.start, self.shape = array, start, (rows, array.shape[1])
        self.dtype = array.dtype

    def __getitem__(self, cut):
        first, last, _ = cut.indices(self.shape[0])
        return Rows(self.array, self.start + first, last - first)

    def value(self):
        if self.shape[0] == self.array.shape[0]:
            return self.array
        return self.array[self.start : self.start + self.shape[0]]


def value(block):
    return block.value() if isinstance(block, Rows) else block


def located(block):
    return (block.array, block.start) if isinstance(block, Rows) else (block, 0)


class Links:
    def __init__(self):
        self.phase = 0
        self.due = {}
        self.queue = {}

    def add(self, block, held, key, lag=1, **hop):
        kind = (tuple(sorted(hop.items())), lag, block.dtype, block.shape[-1])
        group = self.queue.setdefault(kind, [])
        group.append((block, held, key))

    def run(self, others=()):
        groups = list(self.queue.items())
        blocks = [
            jnp.concatenate([value(b) for b, _, _ in moves]) if len(moves) > 1 else value(moves[0][0])
            for _, moves in groups
        ]
        self.last = []
        blocks, _ = lax.optimization_barrier(
            (blocks, self.due.pop(self.phase, []) + list(others))
        )
        for block, ((hop, lag, _, _), moves) in zip(blocks, groups):
            result = send(block, **dict(hop))
            self.due.setdefault(self.phase + lag, []).append(result)
            if lag == 1:
                self.last.append(result)
            start = 0
            for sent, held, key in moves:
                rows = sent.shape[0]
                held[key] = Rows(result, start, rows)
                start += rows
        self.phase += 1
        self.queue = {}


class Spread:
    def __init__(self):
        self.rows, self.ins, self.grads = {}, {}, {}

    def both(self, key):
        self.ins[key], self.grads[key] = self.rows[key][:CAP], self.rows[key][CAP:]

    def first(self, links):
        rows = self.rows
        self.both((0, 0))
        links.add(rows[0, 0], rows, (3, 0), **PLUS)
        links.add(rows[0, 0], rows, (1, 0), **MINUS)
        links.add(rows[0, 0], rows, (0, 1), **CROSS)

    def second(self, links):
        ins, grads = self.ins, self.grads
        for key in ((3, 0), (1, 0), (0, 1)):
            self.both(key)
        links.add(ins[3, 0], ins, (2, 0), **PLUS)
        links.add(ins[0, 1], ins, (3, 1), **PLUS)
        links.add(grads[1, 0], grads, (2, 0), **MINUS)
        links.add(ins[0, 1], ins, (1, 1), **MINUS)
        links.add(grads[1, 0], grads, (1, 1), **CROSS)
        links.add(grads[3, 0], grads, (3, 1), **CROSS)

    def third(self, links):
        links.add(self.ins[3, 1], self.ins, (2, 1), **PLUS)
        links.add(self.grads[1, 1], self.grads, (2, 1), **MINUS)


def added(*parts):
    total = value(parts[0]).astype(jnp.float32)
    for part in parts[1:]:
        total = total + value(part).astype(jnp.float32)
    return total.astype(jnp.bfloat16)


class LateCross:
    def __init__(self, terms):
        self.terms, self.got = terms, {}

    def first(self, links):
        links.add(self.terms[2, 0], self.got, "far+", **PLUS)
        links.add(self.terms[2, 1], self.got, "far-", **MINUS)

    def second(self, links):
        terms, got = self.terms, self.got
        links.add(added(terms[1, 0], got["far+"]), got, "a+", **PLUS)
        links.add(terms[1, 1], got, "b+", **PLUS)
        links.add(terms[3, 0], got, "a-", **MINUS)
        links.add(added(terms[3, 1], got["far-"]), got, "b-", **MINUS)

    def third(self, links):
        got = self.got
        links.add(added(self.terms[0, 1], got["b+"], got["b-"]), got, "z", **CROSS)

    def total(self):
        got = self.got
        return added(self.terms[0, 0], got["a+"], got["a-"], got["z"])


class SoonCross:
    def __init__(self, terms):
        self.terms, self.got = terms, {}

    def first(self, links):
        for dy in range(NY):
            links.add(self.terms[dy, 1], self.got, dy, **CROSS)

    def second(self, links):
        got = self.got
        half = CAP // 2
        self.sums = [added(self.terms[dy, 0], got[dy]) for dy in range(NY)]
        links.add(self.sums[2][:half], got, "far+", **PLUS)
        links.add(self.sums[2][half:], got, "far-", **MINUS)

    def third(self, links):
        sums, got = self.sums, self.got
        half = CAP // 2
        links.add(
            jnp.concatenate([added(sums[1][:half], got["far+"]), sums[1][half:]]),
            got,
            "+",
            **PLUS,
        )
        links.add(
            jnp.concatenate([sums[3][:half], added(sums[3][half:], got["far-"])]),
            got,
            "-",
            **MINUS,
        )

    def total(self):
        return added(self.sums[0], self.got["+"], self.got["-"])


def distinct(pieces):
    arrays = []
    for array, _ in pieces:
        if not any(array is other for other in arrays):
            arrays.append(array)
    return arrays


def index_of(arrays, array):
    return next(i for i, other in enumerate(arrays) if other is array)


def experts_backward(piece, in_pieces, grad_pieces, gate_mat, up_mat, down_mat):
    arrays = distinct(in_pieces + grad_pieces)
    in_plan = [(index_of(arrays, a), r) for a, r in in_pieces]
    grad_plan = [(index_of(arrays, a), r) for a, r in grad_pieces]
    depth, units = gate_mat.shape
    rows = len(in_pieces) * CAP
    step = 1024 if depth % 1024 == 0 else 128

    def kernel(piece_ref, *refs):
        ins = refs[: len(arrays)]
        gate_ref, up_ref, down_ref, out_ref, x_ref, g_ref, a_ref, u_ref, h_ref = refs[
            len(arrays) :
        ]
        a_ref[...] = jnp.zeros_like(a_ref)
        u_ref[...] = jnp.zeros_like(u_ref)
        h_ref[...] = jnp.zeros_like(h_ref)

        @pl.loop(0, depth // step)
        def _(i):
            cols = pl.ds(pl.multiple_of(i * step, step), step)
            for n, (a, r) in enumerate(in_plan):
                x_ref[pl.ds(n * CAP, CAP), :] = ins[a][pl.ds(r, CAP), cols]
            for n, (a, r) in enumerate(grad_plan):
                g_ref[pl.ds(n * CAP, CAP), :] = ins[a][pl.ds(r, CAP), cols]
            x = x_ref[...]
            a_ref[...] += jnp.dot(x, gate_ref[cols, :], preferred_element_type=jnp.float32)
            u_ref[...] += jnp.dot(x, up_ref[cols, :], preferred_element_type=jnp.float32)
            h_ref[...] += lax.dot_general(
                g_ref[...],
                down_ref[:, cols],
                (((1,), (1,)), ((), ())),
                preferred_element_type=jnp.float32,
            )

        gate_pre, up_pre, hidden_grad = a_ref[...], u_ref[...], h_ref[...]
        sigma = jax.nn.sigmoid(gate_pre)
        swish = gate_pre * sigma
        score = jnp.sum(swish * up_pre * hidden_grad, axis=1, keepdims=True)
        gate_back = (hidden_grad * up_pre * sigma * (1.0 + gate_pre * (1.0 - sigma))).astype(
            jnp.bfloat16
        )
        up_back = (hidden_grad * swish).astype(jnp.bfloat16)
        lane = lax.broadcasted_iota(jnp.int32, (rows, MARKS), 1)
        marks = jnp.where(lane == piece_ref[0], score, 0.0)
        out_ref[:, pl.ds(depth, MARKS)] = marks.astype(jnp.bfloat16)

        @pl.loop(0, depth // step)
        def _(i):
            cols = pl.ds(pl.multiple_of(i * step, step), step)
            term = lax.dot_general(
                gate_back,
                gate_ref[cols, :],
                (((1,), (1,)), ((), ())),
                preferred_element_type=jnp.float32,
            )
            term = term + lax.dot_general(
                up_back,
                up_ref[cols, :],
                (((1,), (1,)), ((), ())),
                preferred_element_type=jnp.float32,
            )
            out_ref[:, cols] = term.astype(jnp.bfloat16)

    return pl.pallas_call(
        kernel,
        out_shape=jax.ShapeDtypeStruct((rows, depth + MARKS), jnp.bfloat16),
        in_specs=[SMEM] + [VMEM] * (len(arrays) + 3),
        out_specs=VMEM,
        scratch_shapes=[
            pltpu.VMEM((rows, step), jnp.bfloat16),
            pltpu.VMEM((rows, step), jnp.bfloat16),
            pltpu.VMEM((rows, units), jnp.float32),
            pltpu.VMEM((rows, units), jnp.float32),
            pltpu.VMEM((rows, units), jnp.float32),
        ],
        cost_estimate=pl.CostEstimate(
            flops=FLOPS * rows * depth * units,
            bytes_accessed=2 * (3 * depth * units + 3 * rows * depth),
            transcendentals=rows * units,
        ),
    )(piece, *arrays, gate_mat, up_mat, down_mat)


def blend(base, mix, rows):
    tokens, width = base.shape
    step = 1024 if width % 1024 == 0 else 128

    def kernel(base_ref, mix_ref, *refs):
        out_ref = refs[-1]
        total = base_ref[...].astype(jnp.float32)
        for n, row_ref in enumerate(refs[:-1]):
            weight = mix_ref[:, n * CAP : (n + 1) * CAP]
            high = weight.astype(jnp.bfloat16)
            low = (weight - high.astype(jnp.float32)).astype(jnp.bfloat16)
            for part in (high, low):
                total = total + jnp.dot(part, row_ref[...], preferred_element_type=jnp.float32)
        out_ref[...] = total

    return pl.pallas_call(
        kernel,
        grid=(width // step,),
        out_shape=jax.ShapeDtypeStruct((tokens, width), jnp.float32),
        in_specs=[
            pl.BlockSpec((tokens, step), lambda i: (0, i)),
            pl.BlockSpec(mix.shape, lambda i: (0, 0)),
        ]
        + [pl.BlockSpec((CAP, step), lambda i: (0, i))] * len(rows),
        out_specs=pl.BlockSpec((tokens, step), lambda i: (0, i)),
        cost_estimate=pl.CostEstimate(flops=BLEND, bytes_accessed=8 * tokens * width, transcendentals=0),
    )(base, mix, *rows)


def body(
    layer_input, out_grad, route_ids, route_gates, gate_weight, up_weight, down_weight, head_grad
):
    holder = lax.axis_index("expert")
    group = holder // (NY * NZ)
    piece = (holder % (NY * NZ)).astype(jnp.int32).reshape(1)
    tokens = layer_input[0]
    width = tokens.shape[1]
    grads = out_grad[0]
    routes = route_ids[0]
    gates = route_gates[0]
    weights = gate_weight[0, 0], up_weight[0, 0], down_weight[0, 0]
    order = (jnp.arange(NX, dtype=jnp.int32) + group) % NX
    named = routes[:, :, None] == order[None, None, :]
    hits = jnp.any(named, axis=1).astype(jnp.int32)
    places = jnp.cumsum(hits, axis=0) - hits
    chosen = (places[:, :, None] == jnp.arange(CAP, dtype=jnp.int32)) & (hits[:, :, None] == 1)
    picker = chosen.astype(jnp.bfloat16)
    token_rows = jnp.einsum(
        "tec,td->ecd", picker, tokens, preferred_element_type=jnp.float32
    ).astype(jnp.bfloat16)
    grad_rows = jnp.einsum("tec,td->ecd", picker, grads, preferred_element_type=jnp.float32).astype(
        jnp.bfloat16
    )
    weighted_gate = jnp.sum(gates[:, :, None] * named.astype(jnp.float32), axis=1)
    chosen_float = chosen.astype(jnp.float32)
    mixing = (chosen_float * weighted_gate[:, :, None]).reshape(-1, NX * CAP)

    units = [Spread() for _ in range(NX)]
    rows = [jnp.concatenate([token_rows[dx], grad_rows[dx]]) for dx in range(NX)]
    back, moved, scores = {}, {}, {}
    units[0].rows[0, 0] = Rows(rows[0], 0, 2 * CAP)
    for dx in (1, 3):
        units[dx].rows[0, 0] = Rows(send(rows[dx], dx=dx), 0, 2 * CAP)

    def compute(dxs, kinds):
        ins = [located(units[dx].ins[k]) for dx in dxs for k in BLOCKS]
        gs = [located(units[dx].grads[k]) for dx in dxs for k in BLOCKS]
        term = experts_backward(piece, ins, gs, *weights)
        term = term.reshape(len(dxs), len(BLOCKS), CAP, -1)
        return [
            kind({k: term[i, n] for n, k in enumerate(BLOCKS)}) for i, kind in enumerate(kinds)
        ]

    def home(links, dx, reduced):
        part = reduced.total()
        marks = part[:, width:]
        if dx:
            links.add(marks, scores, dx, dx=-dx)
        else:
            scores[dx] = marks
        links.add(part[:, :width], moved, dx, dx=-dx, back=1)

    def chain(dxs):
        links = Links()
        one, two = (units[dx] for dx in dxs)
        one.first(links)
        if 2 in dxs:
            links.add(rows[2], units[2].rows, (0, 0), dx=2)
        yield links
        two.first(links)
        one.second(links)
        if 0 in dxs:
            links.add(grads, back, "grads", lag=3, back=1)
            links.add(mixing, back, "mixing", lag=3, back=1)
        yield links
        two.second(links)
        one.third(links)
        yield links
        two.third(links)
        yield links
        sums = compute(dxs, [LateCross, SoonCross])
        for part in sums:
            part.first(links)
        yield links
        for part in sums:
            part.second(links)
        yield links
        for part in sums:
            part.third(links)
        yield links
        for dx, part in zip(dxs, sums):
            home(links, dx, part)
        yield links

    for phase, (early, late) in enumerate(zip(chain((0, 1)), chain((3, 2)))):
        early.run()
        late.run(early.last if phase in TIED else ())

    mix = value(back["mixing"])
    early = blend(value(back["grads"]), mix[:, : 2 * CAP], [value(moved[dx]) for dx in (0, 1)])
    sums = jnp.concatenate([value(moved[dx]) for dx in (2, 3)])
    mix = mix[:, 2 * CAP :]
    high = lax.reduce_precision(mix, 8, 7)
    moe_grad = jnp.dot(
        high.astype(jnp.bfloat16), sums, preferred_element_type=jnp.float32
    ) + jnp.dot((mix - high).astype(jnp.bfloat16), sums, preferred_element_type=jnp.float32)
    passed = (early + moe_grad).astype(jnp.bfloat16)
    last_section = lax.axis_index("pipe") == lax.axis_size("pipe") - 1
    next_grad = jnp.where(last_section, head_grad, passed)

    totals = jnp.sum(jnp.stack([value(scores[dx]) for dx in range(NX)]).astype(jnp.float32), axis=2)
    token_scores = jnp.sum(chosen_float * totals[None], axis=2)
    gate_grad = jnp.sum(named.astype(jnp.float32) * token_scores[:, None, :], axis=2)
    return (next_grad[None], gate_grad[None])


def solution(mesh):
    in_specs = (
        P("pipe", "expert", None),
        P("pipe", "expert", None),
        P("pipe", "expert", None),
        P("pipe", "expert", None),
        P("pipe", "expert", None, None),
        P("pipe", "expert", None, None),
        P("pipe", "expert", None, None),
        P("expert", None),
    )
    out_specs = (P("pipe", "expert", None), P("pipe", "expert", None))
    return jax.shard_map(body, mesh=mesh, in_specs=in_specs, out_specs=out_specs, check_vma=False)
```

```python
import jax
import jax.numpy as jnp
from jax import lax
from jax.experimental import pallas as pl
from jax.experimental.pallas import tpu as pltpu
from jax.sharding import PartitionSpec as P

CAP = 16
MARKS = 128
NX, NY, NZ = 4, 4, 2
FLOPS = 40
HOME = 7
BLEND = 25000000000
VMEM = pl.BlockSpec(memory_space=pltpu.VMEM)
SMEM = pl.BlockSpec(memory_space=pltpu.SMEM)
BLOCKS = [(dy, dz) for dz in range(NZ) for dy in range(NY)]
PLUS, MINUS, CROSS = dict(dy=1), dict(dy=-1), dict(dz=1)


def place(x, y, z):
    return ((x % NX) * NY + y % NY) * NZ + z % NZ


def send(block, dx=0, dy=0, dz=0, back=0):
    route = []
    for x in range(NX):
        for y in range(NY):
            for z in range(NZ):
                route.append((place(x, y, z), place(x + dx, y + dy, z + dz)))
    if not back:
        return lax.ppermute(block, "expert", route)
    size = NX * NY * NZ
    route = [
        (p * size + i, (p - back) * size + j)
        for p in range(back, lax.axis_size("pipe"))
        for i, j in route
    ]
    return lax.ppermute(block, ("pipe", "expert"), route)


class Rows:
    def __init__(self, array, start, rows):
        self.array, self.start, self.shape = array, start, (rows, array.shape[1])
        self.dtype = array.dtype

    def __getitem__(self, cut):
        first, last, _ = cut.indices(self.shape[0])
        return Rows(self.array, self.start + first, last - first)

    def value(self):
        if self.shape[0] == self.array.shape[0]:
            return self.array
        return self.array[self.start : self.start + self.shape[0]]


def value(block):
    return block.value() if isinstance(block, Rows) else block


def located(block):
    return (block.array, block.start) if isinstance(block, Rows) else (block, 0)


class Links:
    def __init__(self):
        self.phase = 0
        self.due = {}
        self.queue = {}

    def add(self, block, held, key, lag=1, **hop):
        kind = (tuple(sorted(hop.items())), lag, block.dtype, block.shape[-1])
        group = self.queue.setdefault(kind, [])
        group.append((block, held, key))

    def run(self, others=()):
        groups = list(self.queue.items())
        blocks = [
            jnp.concatenate([value(b) for b, _, _ in moves]) if len(moves) > 1 else value(moves[0][0])
            for _, moves in groups
        ]
        self.last = []
        blocks, _ = lax.optimization_barrier(
            (blocks, self.due.pop(self.phase, []) + list(others))
        )
        for block, ((hop, lag, _, _), moves) in zip(blocks, groups):
            result = send(block, **dict(hop))
            self.due.setdefault(self.phase + lag, []).append(result)
            if lag == 1:
                self.last.append(result)
            start = 0
            for sent, held, key in moves:
                rows = sent.shape[0]
                held[key] = Rows(result, start, rows)
                start += rows
        self.phase += 1
        self.queue = {}


class Spread:
    def __init__(self):
        self.rows, self.ins, self.grads = {}, {}, {}

    def both(self, key):
        self.ins[key], self.grads[key] = self.rows[key][:CAP], self.rows[key][CAP:]

    def first(self, links):
        rows = self.rows
        self.both((0, 0))
        links.add(rows[0, 0], rows, (3, 0), **PLUS)
        links.add(rows[0, 0], rows, (1, 0), **MINUS)
        links.add(rows[0, 0], rows, (0, 1), **CROSS)

    def second(self, links):
        ins, grads = self.ins, self.grads
        for key in ((3, 0), (1, 0), (0, 1)):
            self.both(key)
        links.add(ins[3, 0], ins, (2, 0), **PLUS)
        links.add(ins[0, 1], ins, (3, 1), **PLUS)
        links.add(grads[1, 0], grads, (2, 0), **MINUS)
        links.add(ins[0, 1], ins, (1, 1), **MINUS)
        links.add(grads[1, 0], grads, (1, 1), **CROSS)
        links.add(grads[3, 0], grads, (3, 1), **CROSS)

    def third(self, links):
        links.add(self.ins[3, 1], self.ins, (2, 1), **PLUS)
        links.add(self.grads[1, 1], self.grads, (2, 1), **MINUS)


def added(*parts):
    total = value(parts[0]).astype(jnp.float32)
    for part in parts[1:]:
        total = total + value(part).astype(jnp.float32)
    return total.astype(jnp.bfloat16)


class LateCross:
    def __init__(self, terms):
        self.terms, self.got = terms, {}

    def first(self, links):
        links.add(self.terms[2, 0], self.got, "far+", **PLUS)
        links.add(self.terms[2, 1], self.got, "far-", **MINUS)

    def second(self, links):
        terms, got = self.terms, self.got
        links.add(added(terms[1, 0], got["far+"]), got, "a+", **PLUS)
        links.add(terms[1, 1], got, "b+", **PLUS)
        links.add(terms[3, 0], got, "a-", **MINUS)
        links.add(added(terms[3, 1], got["far-"]), got, "b-", **MINUS)

    def third(self, links):
        got = self.got
        links.add(added(self.terms[0, 1], got["b+"], got["b-"]), got, "z", **CROSS)

    def total(self):
        got = self.got
        return added(self.terms[0, 0], got["a+"], got["a-"], got["z"])


class SoonCross:
    def __init__(self, terms):
        self.terms, self.got = terms, {}

    def first(self, links):
        for dy in range(NY):
            links.add(self.terms[dy, 1], self.got, dy, **CROSS)

    def second(self, links):
        got = self.got
        half = CAP // 2
        self.sums = [added(self.terms[dy, 0], got[dy]) for dy in range(NY)]
        links.add(self.sums[2][:half], got, "far+", **PLUS)
        links.add(self.sums[2][half:], got, "far-", **MINUS)

    def third(self, links):
        sums, got = self.sums, self.got
        half = CAP // 2
        links.add(
            jnp.concatenate([added(sums[1][:half], got["far+"]), sums[1][half:]]),
            got,
            "+",
            **PLUS,
        )
        links.add(
            jnp.concatenate([sums[3][:half], added(sums[3][half:], got["far-"])]),
            got,
            "-",
            **MINUS,
        )

    def total(self):
        return added(self.sums[0], self.got["+"], self.got["-"])


def distinct(pieces):
    arrays = []
    for array, _ in pieces:
        if not any(array is other for other in arrays):
            arrays.append(array)
    return arrays


def index_of(arrays, array):
    return next(i for i, other in enumerate(arrays) if other is array)


def experts_backward(piece, in_pieces, grad_pieces, gate_mat, up_mat, down_mat):
    arrays = distinct(in_pieces + grad_pieces)
    in_plan = [(index_of(arrays, a), r) for a, r in in_pieces]
    grad_plan = [(index_of(arrays, a), r) for a, r in grad_pieces]
    depth, units = gate_mat.shape
    rows = len(in_pieces) * CAP
    step = 1024 if depth % 1024 == 0 else 128

    def kernel(piece_ref, *refs):
        ins = refs[: len(arrays)]
        gate_ref, up_ref, down_ref, out_ref, x_ref, g_ref, a_ref, u_ref, h_ref = refs[
            len(arrays) :
        ]
        a_ref[...] = jnp.zeros_like(a_ref)
        u_ref[...] = jnp.zeros_like(u_ref)
        h_ref[...] = jnp.zeros_like(h_ref)

        @pl.loop(0, depth // step)
        def _(i):
            cols = pl.ds(pl.multiple_of(i * step, step), step)
            for n, (a, r) in enumerate(in_plan):
                x_ref[pl.ds(n * CAP, CAP), :] = ins[a][pl.ds(r, CAP), cols]
            for n, (a, r) in enumerate(grad_plan):
                g_ref[pl.ds(n * CAP, CAP), :] = ins[a][pl.ds(r, CAP), cols]
            x = x_ref[...]
            a_ref[...] += jnp.dot(x, gate_ref[cols, :], preferred_element_type=jnp.float32)
            u_ref[...] += jnp.dot(x, up_ref[cols, :], preferred_element_type=jnp.float32)
            h_ref[...] += lax.dot_general(
                g_ref[...],
                down_ref[:, cols],
                (((1,), (1,)), ((), ())),
                preferred_element_type=jnp.float32,
            )

        gate_pre, up_pre, hidden_grad = a_ref[...], u_ref[...], h_ref[...]
        sigma = jax.nn.sigmoid(gate_pre)
        swish = gate_pre * sigma
        score = jnp.sum(swish * up_pre * hidden_grad, axis=1, keepdims=True)
        gate_back = (hidden_grad * up_pre * sigma * (1.0 + gate_pre * (1.0 - sigma))).astype(
            jnp.bfloat16
        )
        up_back = (hidden_grad * swish).astype(jnp.bfloat16)
        lane = lax.broadcasted_iota(jnp.int32, (rows, MARKS), 1)
        marks = jnp.where(lane == piece_ref[0], score, 0.0)
        out_ref[:, pl.ds(depth, MARKS)] = marks.astype(jnp.bfloat16)

        @pl.loop(0, depth // step)
        def _(i):
            cols = pl.ds(pl.multiple_of(i * step, step), step)
            term = lax.dot_general(
                gate_back,
                gate_ref[cols, :],
                (((1,), (1,)), ((), ())),
                preferred_element_type=jnp.float32,
            )
            term = term + lax.dot_general(
                up_back,
                up_ref[cols, :],
                (((1,), (1,)), ((), ())),
                preferred_element_type=jnp.float32,
            )
            out_ref[:, cols] = term.astype(jnp.bfloat16)

    return pl.pallas_call(
        kernel,
        out_shape=jax.ShapeDtypeStruct((rows, depth + MARKS), jnp.bfloat16),
        in_specs=[SMEM] + [VMEM] * (len(arrays) + 3),
        out_specs=VMEM,
        scratch_shapes=[
            pltpu.VMEM((rows, step), jnp.bfloat16),
            pltpu.VMEM((rows, step), jnp.bfloat16),
            pltpu.VMEM((rows, units), jnp.float32),
            pltpu.VMEM((rows, units), jnp.float32),
            pltpu.VMEM((rows, units), jnp.float32),
        ],
        cost_estimate=pl.CostEstimate(
            flops=FLOPS * rows * depth * units,
            bytes_accessed=2 * (3 * depth * units + 3 * rows * depth),
            transcendentals=rows * units,
        ),
    )(piece, *arrays, gate_mat, up_mat, down_mat)


def blend(base, mix, rows):
    tokens, width = base.shape
    step = 1024 if width % 1024 == 0 else 128

    def kernel(base_ref, mix_ref, *refs):
        out_ref = refs[-1]
        total = base_ref[...].astype(jnp.float32)
        for n, row_ref in enumerate(refs[:-1]):
            weight = mix_ref[:, n * CAP : (n + 1) * CAP]
            high = weight.astype(jnp.bfloat16)
            low = (weight - high.astype(jnp.float32)).astype(jnp.bfloat16)
            for part in (high, low):
                total = total + jnp.dot(part, row_ref[...], preferred_element_type=jnp.float32)
        out_ref[...] = total

    return pl.pallas_call(
        kernel,
        grid=(width // step,),
        out_shape=jax.ShapeDtypeStruct((tokens, width), jnp.float32),
        in_specs=[
            pl.BlockSpec((tokens, step), lambda i: (0, i)),
            pl.BlockSpec(mix.shape, lambda i: (0, 0)),
        ]
        + [pl.BlockSpec((CAP, step), lambda i: (0, i))] * len(rows),
        out_specs=pl.BlockSpec((tokens, step), lambda i: (0, i)),
        cost_estimate=pl.CostEstimate(flops=BLEND, bytes_accessed=8 * tokens * width, transcendentals=0),
    )(base, mix, *rows)


def body(
    layer_input, out_grad, route_ids, route_gates, gate_weight, up_weight, down_weight, head_grad
):
    holder = lax.axis_index("expert")
    group = holder // (NY * NZ)
    piece = (holder % (NY * NZ)).astype(jnp.int32).reshape(1)
    tokens = layer_input[0]
    width = tokens.shape[1]
    grads = out_grad[0]
    routes = route_ids[0]
    gates = route_gates[0]
    weights = gate_weight[0, 0], up_weight[0, 0], down_weight[0, 0]
    order = (jnp.arange(NX, dtype=jnp.int32) + group) % NX
    named = routes[:, :, None] == order[None, None, :]
    hits = jnp.any(named, axis=1).astype(jnp.int32)
    places = jnp.cumsum(hits, axis=0) - hits
    chosen = (places[:, :, None] == jnp.arange(CAP, dtype=jnp.int32)) & (hits[:, :, None] == 1)
    picker = chosen.astype(jnp.bfloat16)
    token_rows = jnp.einsum(
        "tec,td->ecd", picker, tokens, preferred_element_type=jnp.float32
    ).astype(jnp.bfloat16)
    grad_rows = jnp.einsum("tec,td->ecd", picker, grads, preferred_element_type=jnp.float32).astype(
        jnp.bfloat16
    )
    weighted_gate = jnp.sum(gates[:, :, None] * named.astype(jnp.float32), axis=1)
    chosen_float = chosen.astype(jnp.float32)
    mixing = (chosen_float * weighted_gate[:, :, None]).reshape(-1, NX * CAP)

    units = [Spread() for _ in range(NX)]
    rows = [jnp.concatenate([token_rows[dx], grad_rows[dx]]) for dx in range(NX)]
    back, moved, scores = {}, {}, {}
    units[0].rows[0, 0] = Rows(rows[0], 0, 2 * CAP)
    for dx in (1, 3):
        units[dx].rows[0, 0] = Rows(send(rows[dx], dx=dx), 0, 2 * CAP)

    def compute(dxs, kinds):
        ins = [located(units[dx].ins[k]) for dx in dxs for k in BLOCKS]
        gs = [located(units[dx].grads[k]) for dx in dxs for k in BLOCKS]
        term = experts_backward(piece, ins, gs, *weights)
        term = term.reshape(len(dxs), len(BLOCKS), CAP, -1)
        return [
            kind({k: term[i, n] for n, k in enumerate(BLOCKS)}) for i, kind in enumerate(kinds)
        ]

    def home(links, dx, reduced):
        part = reduced.total()
        marks = part[:, width:]
        if dx:
            links.add(marks, scores, dx, dx=-dx)
        else:
            scores[dx] = marks
        links.add(part[:, :width], moved, dx, dx=-dx, back=1)

    def chain(dxs):
        links = Links()
        one, two = (units[dx] for dx in dxs)
        one.first(links)
        if 2 in dxs:
            links.add(rows[2], units[2].rows, (0, 0), dx=2)
        yield links
        two.first(links)
        one.second(links)
        if 0 in dxs:
            links.add(grads, back, "grads", lag=3, back=1)
            links.add(mixing, back, "mixing", lag=3, back=1)
        yield links
        two.second(links)
        one.third(links)
        yield links
        two.third(links)
        yield links
        sums = compute(dxs, [SoonCross, LateCross] if 0 in dxs else [SoonCross, LateCross])
        for part in sums:
            part.first(links)
        yield links
        for part in sums:
            part.second(links)
        yield links
        for part in sums:
            part.third(links)
        yield links
        for dx, part in zip(dxs, sums):
            home(links, dx, part)
        yield links

    for phase, (early, late) in enumerate(zip(chain((0, 1)), chain((3, 2)))):
        early.run()
        others = ()
        if phase == HOME:
            mix = value(back["mixing"])
            near = [value(moved[dx]) for dx in (0, 1)]
            mixed = blend(value(back["grads"]), mix[:, : 2 * CAP], near)
            others = [mixed]
        late.run(others)

    sums = jnp.concatenate([value(moved[dx]) for dx in (2, 3)])
    mix = mix[:, 2 * CAP :]
    high = lax.reduce_precision(mix, 8, 7)
    moe_grad = jnp.dot(
        high.astype(jnp.bfloat16), sums, preferred_element_type=jnp.float32
    ) + jnp.dot((mix - high).astype(jnp.bfloat16), sums, preferred_element_type=jnp.float32)
    passed = (mixed + moe_grad).astype(jnp.bfloat16)
    last_section = lax.axis_index("pipe") == lax.axis_size("pipe") - 1
    next_grad = jnp.where(last_section, head_grad, passed)

    totals = jnp.sum(jnp.stack([value(scores[dx]) for dx in range(NX)]).astype(jnp.float32), axis=2)
    token_scores = jnp.sum(chosen_float * totals[None], axis=2)
    gate_grad = jnp.sum(named.astype(jnp.float32) * token_scores[:, None, :], axis=2)
    return (next_grad[None], gate_grad[None])


def solution(mesh):
    in_specs = (
        P("pipe", "expert", None),
        P("pipe", "expert", None),
        P("pipe", "expert", None),
        P("pipe", "expert", None),
        P("pipe", "expert", None, None),
        P("pipe", "expert", None, None),
        P("pipe", "expert", None, None),
        P("expert", None),
    )
    out_specs = (P("pipe", "expert", None), P("pipe", "expert", None))
    return jax.shard_map(body, mesh=mesh, in_specs=in_specs, out_specs=out_specs, check_vma=False)
```

```python
import jax
import jax.numpy as jnp
from jax import lax
from jax.experimental import pallas as pl
from jax.experimental.pallas import tpu as pltpu
from jax.sharding import PartitionSpec as P

CAP = 16
MARKS = 128
NX, NY, NZ = 4, 4, 2
FLOPS = 40
HOME = 7
BLEND = 25000000000
VMEM = pl.BlockSpec(memory_space=pltpu.VMEM)
SMEM = pl.BlockSpec(memory_space=pltpu.SMEM)
BLOCKS = [(dy, dz) for dz in range(NZ) for dy in range(NY)]
PLUS, MINUS, CROSS = dict(dy=1), dict(dy=-1), dict(dz=1)


def place(x, y, z):
    return ((x % NX) * NY + y % NY) * NZ + z % NZ


def send(block, dx=0, dy=0, dz=0, back=0):
    route = []
    for x in range(NX):
        for y in range(NY):
            for z in range(NZ):
                route.append((place(x, y, z), place(x + dx, y + dy, z + dz)))
    if not back:
        return lax.ppermute(block, "expert", route)
    size = NX * NY * NZ
    route = [
        (p * size + i, (p - back) * size + j)
        for p in range(back, lax.axis_size("pipe"))
        for i, j in route
    ]
    return lax.ppermute(block, ("pipe", "expert"), route)


class Rows:
    def __init__(self, array, start, rows):
        self.array, self.start, self.shape = array, start, (rows, array.shape[1])
        self.dtype = array.dtype

    def __getitem__(self, cut):
        first, last, _ = cut.indices(self.shape[0])
        return Rows(self.array, self.start + first, last - first)

    def value(self):
        if self.shape[0] == self.array.shape[0]:
            return self.array
        return self.array[self.start : self.start + self.shape[0]]


def value(block):
    return block.value() if isinstance(block, Rows) else block


def located(block):
    return (block.array, block.start) if isinstance(block, Rows) else (block, 0)


class Links:
    def __init__(self):
        self.phase = 0
        self.due = {}
        self.queue = {}

    def add(self, block, held, key, lag=1, **hop):
        kind = (tuple(sorted(hop.items())), lag, block.dtype, block.shape[-1])
        group = self.queue.setdefault(kind, [])
        group.append((block, held, key))

    def run(self, others=()):
        groups = list(self.queue.items())
        blocks = [
            jnp.concatenate([value(b) for b, _, _ in moves]) if len(moves) > 1 else value(moves[0][0])
            for _, moves in groups
        ]
        self.last = []
        blocks, _ = lax.optimization_barrier(
            (blocks, self.due.pop(self.phase, []) + list(others))
        )
        for block, ((hop, lag, _, _), moves) in zip(blocks, groups):
            result = send(block, **dict(hop))
            self.due.setdefault(self.phase + lag, []).append(result)
            if lag == 1:
                self.last.append(result)
            start = 0
            for sent, held, key in moves:
                rows = sent.shape[0]
                held[key] = Rows(result, start, rows)
                start += rows
        self.phase += 1
        self.queue = {}


class Spread:
    def __init__(self):
        self.rows, self.ins, self.grads = {}, {}, {}

    def both(self, key):
        self.ins[key], self.grads[key] = self.rows[key][:CAP], self.rows[key][CAP:]

    def first(self, links):
        rows = self.rows
        self.both((0, 0))
        links.add(rows[0, 0], rows, (3, 0), **PLUS)
        links.add(rows[0, 0], rows, (1, 0), **MINUS)
        links.add(rows[0, 0], rows, (0, 1), **CROSS)

    def second(self, links):
        ins, grads = self.ins, self.grads
        for key in ((3, 0), (1, 0), (0, 1)):
            self.both(key)
        links.add(ins[3, 0], ins, (2, 0), **PLUS)
        links.add(ins[0, 1], ins, (3, 1), **PLUS)
        links.add(grads[1, 0], grads, (2, 0), **MINUS)
        links.add(ins[0, 1], ins, (1, 1), **MINUS)
        links.add(grads[1, 0], grads, (1, 1), **CROSS)
        links.add(grads[3, 0], grads, (3, 1), **CROSS)

    def third(self, links):
        links.add(self.ins[3, 1], self.ins, (2, 1), **PLUS)
        links.add(self.grads[1, 1], self.grads, (2, 1), **MINUS)


def added(*parts):
    total = value(parts[0]).astype(jnp.float32)
    for part in parts[1:]:
        total = total + value(part).astype(jnp.float32)
    return total.astype(jnp.bfloat16)


class LateCross:
    def __init__(self, terms):
        self.terms, self.got = terms, {}

    def first(self, links):
        links.add(self.terms[2, 0], self.got, "far+", **PLUS)
        links.add(self.terms[2, 1], self.got, "far-", **MINUS)

    def second(self, links):
        terms, got = self.terms, self.got
        links.add(added(terms[1, 0], got["far+"]), got, "a+", **PLUS)
        links.add(terms[1, 1], got, "b+", **PLUS)
        links.add(terms[3, 0], got, "a-", **MINUS)
        links.add(added(terms[3, 1], got["far-"]), got, "b-", **MINUS)

    def third(self, links):
        got = self.got
        links.add(added(self.terms[0, 1], got["b+"], got["b-"]), got, "z", **CROSS)

    def total(self):
        got = self.got
        return added(self.terms[0, 0], got["a+"], got["a-"], got["z"])


class SoonCross:
    def __init__(self, terms):
        self.terms, self.got = terms, {}

    def first(self, links):
        for dy in range(NY):
            links.add(self.terms[dy, 1], self.got, dy, **CROSS)

    def second(self, links):
        got = self.got
        half = CAP // 2
        self.sums = [added(self.terms[dy, 0], got[dy]) for dy in range(NY)]
        links.add(self.sums[2][:half], got, "far+", **PLUS)
        links.add(self.sums[2][half:], got, "far-", **MINUS)

    def third(self, links):
        sums, got = self.sums, self.got
        half = CAP // 2
        links.add(
            jnp.concatenate([added(sums[1][:half], got["far+"]), sums[1][half:]]),
            got,
            "+",
            **PLUS,
        )
        links.add(
            jnp.concatenate([sums[3][:half], added(sums[3][half:], got["far-"])]),
            got,
            "-",
            **MINUS,
        )

    def total(self):
        return added(self.sums[0], self.got["+"], self.got["-"])


def distinct(pieces):
    arrays = []
    for array, _ in pieces:
        if not any(array is other for other in arrays):
            arrays.append(array)
    return arrays


def index_of(arrays, array):
    return next(i for i, other in enumerate(arrays) if other is array)


def experts_backward(piece, in_pieces, grad_pieces, gate_mat, up_mat, down_mat):
    arrays = distinct(in_pieces + grad_pieces)
    in_plan = [(index_of(arrays, a), r) for a, r in in_pieces]
    grad_plan = [(index_of(arrays, a), r) for a, r in grad_pieces]
    depth, units = gate_mat.shape
    rows = len(in_pieces) * CAP
    step = 1792 if depth % 1792 == 0 else 128

    def kernel(piece_ref, *refs):
        ins = refs[: len(arrays)]
        gate_ref, up_ref, down_ref, out_ref, x_ref, g_ref, a_ref, u_ref, h_ref = refs[
            len(arrays) :
        ]
        a_ref[...] = jnp.zeros_like(a_ref)
        u_ref[...] = jnp.zeros_like(u_ref)
        h_ref[...] = jnp.zeros_like(h_ref)

        @pl.loop(0, depth // step)
        def _(i):
            cols = pl.ds(pl.multiple_of(i * step, step), step)
            for n, (a, r) in enumerate(in_plan):
                x_ref[pl.ds(n * CAP, CAP), :] = ins[a][pl.ds(r, CAP), cols]
            for n, (a, r) in enumerate(grad_plan):
                g_ref[pl.ds(n * CAP, CAP), :] = ins[a][pl.ds(r, CAP), cols]
            x = x_ref[...]
            a_ref[...] += jnp.dot(x, gate_ref[cols, :], preferred_element_type=jnp.float32)
            u_ref[...] += jnp.dot(x, up_ref[cols, :], preferred_element_type=jnp.float32)
            h_ref[...] += lax.dot_general(
                g_ref[...],
                down_ref[:, cols],
                (((1,), (1,)), ((), ())),
                preferred_element_type=jnp.float32,
            )

        gate_pre, up_pre, hidden_grad = a_ref[...], u_ref[...], h_ref[...]
        sigma = jax.nn.sigmoid(gate_pre)
        swish = gate_pre * sigma
        score = jnp.sum(swish * up_pre * hidden_grad, axis=1, keepdims=True)
        gate_back = (hidden_grad * up_pre * sigma * (1.0 + gate_pre * (1.0 - sigma))).astype(
            jnp.bfloat16
        )
        up_back = (hidden_grad * swish).astype(jnp.bfloat16)
        lane = lax.broadcasted_iota(jnp.int32, (rows, MARKS), 1)
        marks = jnp.where(lane == piece_ref[0], score, 0.0)
        out_ref[:, pl.ds(depth, MARKS)] = marks.astype(jnp.bfloat16)

        @pl.loop(0, depth // step)
        def _(i):
            cols = pl.ds(pl.multiple_of(i * step, step), step)
            term = lax.dot_general(
                gate_back,
                gate_ref[cols, :],
                (((1,), (1,)), ((), ())),
                preferred_element_type=jnp.float32,
            )
            term = term + lax.dot_general(
                up_back,
                up_ref[cols, :],
                (((1,), (1,)), ((), ())),
                preferred_element_type=jnp.float32,
            )
            out_ref[:, cols] = term.astype(jnp.bfloat16)

    return pl.pallas_call(
        kernel,
        out_shape=jax.ShapeDtypeStruct((rows, depth + MARKS), jnp.bfloat16),
        in_specs=[SMEM] + [VMEM] * (len(arrays) + 3),
        out_specs=VMEM,
        scratch_shapes=[
            pltpu.VMEM((rows, step), jnp.bfloat16),
            pltpu.VMEM((rows, step), jnp.bfloat16),
            pltpu.VMEM((rows, units), jnp.float32),
            pltpu.VMEM((rows, units), jnp.float32),
            pltpu.VMEM((rows, units), jnp.float32),
        ],
        cost_estimate=pl.CostEstimate(
            flops=FLOPS * rows * depth * units,
            bytes_accessed=2 * (3 * depth * units + 3 * rows * depth),
            transcendentals=rows * units,
        ),
    )(piece, *arrays, gate_mat, up_mat, down_mat)


def blend(base, mix, rows):
    tokens, width = base.shape
    step = 1024 if width % 1024 == 0 else 128

    def kernel(base_ref, mix_ref, *refs):
        out_ref = refs[-1]
        total = base_ref[...].astype(jnp.float32)
        for n, row_ref in enumerate(refs[:-1]):
            weight = mix_ref[:, n * CAP : (n + 1) * CAP]
            high = weight.astype(jnp.bfloat16)
            low = (weight - high.astype(jnp.float32)).astype(jnp.bfloat16)
            for part in (high, low):
                total = total + jnp.dot(part, row_ref[...], preferred_element_type=jnp.float32)
        out_ref[...] = total

    return pl.pallas_call(
        kernel,
        grid=(width // step,),
        out_shape=jax.ShapeDtypeStruct((tokens, width), jnp.float32),
        in_specs=[
            pl.BlockSpec((tokens, step), lambda i: (0, i)),
            pl.BlockSpec(mix.shape, lambda i: (0, 0)),
        ]
        + [pl.BlockSpec((CAP, step), lambda i: (0, i))] * len(rows),
        out_specs=pl.BlockSpec((tokens, step), lambda i: (0, i)),
        cost_estimate=pl.CostEstimate(flops=BLEND, bytes_accessed=8 * tokens * width, transcendentals=0),
    )(base, mix, *rows)


def body(
    layer_input, out_grad, route_ids, route_gates, gate_weight, up_weight, down_weight, head_grad
):
    holder = lax.axis_index("expert")
    group = holder // (NY * NZ)
    piece = (holder % (NY * NZ)).astype(jnp.int32).reshape(1)
    tokens = layer_input[0]
    width = tokens.shape[1]
    grads = out_grad[0]
    routes = route_ids[0]
    gates = route_gates[0]
    weights = gate_weight[0, 0], up_weight[0, 0], down_weight[0, 0]
    order = (jnp.arange(NX, dtype=jnp.int32) + group) % NX
    named = routes[:, :, None] == order[None, None, :]
    hits = jnp.any(named, axis=1).astype(jnp.int32)
    places = jnp.cumsum(hits, axis=0) - hits
    chosen = (places[:, :, None] == jnp.arange(CAP, dtype=jnp.int32)) & (hits[:, :, None] == 1)
    picker = chosen.astype(jnp.bfloat16)
    token_rows = jnp.einsum(
        "tec,td->ecd", picker, tokens, preferred_element_type=jnp.float32
    ).astype(jnp.bfloat16)
    grad_rows = jnp.einsum("tec,td->ecd", picker, grads, preferred_element_type=jnp.float32).astype(
        jnp.bfloat16
    )
    weighted_gate = jnp.sum(gates[:, :, None] * named.astype(jnp.float32), axis=1)
    chosen_float = chosen.astype(jnp.float32)
    mixing = (chosen_float * weighted_gate[:, :, None]).reshape(-1, NX * CAP)

    units = [Spread() for _ in range(NX)]
    rows = [jnp.concatenate([token_rows[dx], grad_rows[dx]]) for dx in range(NX)]
    back, moved, scores = {}, {}, {}
    units[0].rows[0, 0] = Rows(rows[0], 0, 2 * CAP)
    for dx in (1, 3):
        units[dx].rows[0, 0] = Rows(send(rows[dx], dx=dx), 0, 2 * CAP)

    def compute(dxs, kinds):
        ins = [located(units[dx].ins[k]) for dx in dxs for k in BLOCKS]
        gs = [located(units[dx].grads[k]) for dx in dxs for k in BLOCKS]
        term = experts_backward(piece, ins, gs, *weights)
        term = term.reshape(len(dxs), len(BLOCKS), CAP, -1)
        return [
            kind({k: term[i, n] for n, k in enumerate(BLOCKS)}) for i, kind in enumerate(kinds)
        ]

    def home(links, dx, reduced):
        part = reduced.total()
        marks = part[:, width:]
        if dx:
            links.add(marks, scores, dx, dx=-dx)
        else:
            scores[dx] = marks
        links.add(part[:, :width], moved, dx, dx=-dx, back=1)

    def chain(dxs):
        links = Links()
        one, two = (units[dx] for dx in dxs)
        one.first(links)
        if 2 in dxs:
            links.add(rows[2], units[2].rows, (0, 0), dx=2)
        yield links
        two.first(links)
        one.second(links)
        if 0 in dxs:
            links.add(grads, back, "grads", lag=3, back=1)
            links.add(mixing, back, "mixing", lag=3, back=1)
        yield links
        two.second(links)
        one.third(links)
        yield links
        two.third(links)
        yield links
        sums = compute(dxs, [SoonCross, LateCross] if 0 in dxs else [SoonCross, LateCross])
        for part in sums:
            part.first(links)
        yield links
        for part in sums:
            part.second(links)
        yield links
        for part in sums:
            part.third(links)
        yield links
        for dx, part in zip(dxs, sums):
            home(links, dx, part)
        yield links

    for phase, (early, late) in enumerate(zip(chain((0, 1)), chain((3, 2)))):
        early.run()
        others = ()
        if phase == HOME:
            mix = value(back["mixing"])
            near = [value(moved[dx]) for dx in (0, 1)]
            mixed = blend(value(back["grads"]), mix[:, : 2 * CAP], near)
            others = [mixed]
        late.run(others)

    sums = jnp.concatenate([value(moved[dx]) for dx in (2, 3)])
    mix = mix[:, 2 * CAP :]
    high = lax.reduce_precision(mix, 8, 7)
    moe_grad = jnp.dot(
        high.astype(jnp.bfloat16), sums, preferred_element_type=jnp.float32
    ) + jnp.dot((mix - high).astype(jnp.bfloat16), sums, preferred_element_type=jnp.float32)
    passed = (mixed + moe_grad).astype(jnp.bfloat16)
    last_section = lax.axis_index("pipe") == lax.axis_size("pipe") - 1
    next_grad = jnp.where(last_section, head_grad, passed)

    totals = jnp.sum(jnp.stack([value(scores[dx]) for dx in range(NX)]).astype(jnp.float32), axis=2)
    token_scores = jnp.sum(chosen_float * totals[None], axis=2)
    gate_grad = jnp.sum(named.astype(jnp.float32) * token_scores[:, None, :], axis=2)
    return (next_grad[None], gate_grad[None])


def solution(mesh):
    in_specs = (
        P("pipe", "expert", None),
        P("pipe", "expert", None),
        P("pipe", "expert", None),
        P("pipe", "expert", None),
        P("pipe", "expert", None, None),
        P("pipe", "expert", None, None),
        P("pipe", "expert", None, None),
        P("expert", None),
    )
    out_specs = (P("pipe", "expert", None), P("pipe", "expert", None))
    return jax.shard_map(body, mesh=mesh, in_specs=in_specs, out_specs=out_specs, check_vma=False)
```
